32 devices in a mesh: feat: 2 (over y), rows: 16 (over z, x, core).
Axes of the slice: x: 2, y: 2, z: 4, core: 2. Of those that a mesh axis runs over, the one named last changes fastest.
Arguments:
- x_vals: bfloat16 [32, 2, 8, 512, 128], P('rows', 'feat'), may hold values from -6 to 6
- x_blocks: int32 [32, 2, 8], P('rows', 'feat'), may hold values from 0 to 783
- y_vals: bfloat16 [16, 2, 8, 512, 128], P('rows', 'feat'), may hold values from -6 to 6
- y_blocks: int32 [16, 2, 8], P('rows', 'feat'), may hold values from 0 to 391
- user_weights: bfloat16 [256, 200704], P('rows', 'feat'), may hold values from -0.125 to 0.125
- item_weights: bfloat16 [256, 100352], P('rows', 'feat'), may hold values from -0.125 to 0.125
- observed: int32 [32, 16], P('rows'), may hold values 0 or 1
- ratings: bfloat16 [16384, 2, 4096], P('rows', 'feat'), may hold values from -6 to 6
Outputs:
- grad_user: float32 [256, 200704], P('rows', 'feat')
- grad_item: float32 [256, 100352], P('rows', 'feat')
The draws below stay inside these ranges and needn't reach their ends.
Inputs may be any that keep to these rules, and one draw needn't show every extreme that they name: `x_blocks`: feature block numbers within one shard. `y_blocks`: feature block numbers within one shard.
All inputs are finite; a program needn't handle non-finite values. No bound on the sum of `observed` on one device may be relied on, other than what follows from the above.
Results may differ from the reference program's by a relative error of at most 0.008.
Values may be sent and summed in bfloat16 or wider, within the bound.
No kernel may reach another device: no remote copies, remote signals or barrier semaphores. Data moves between devices by JAX's collectives and lax.ppermute only.
A program may use at most 64 MiB of HBM per device.

```python
import math
import jax
import jax.numpy as jnp
import numpy as np
from jax import lax

TILE = 512
FBW = 128
RANK = 256
FU = 200704
FI = 100352
KBF = 8
KBI = 8
NUB = 32
NIB = 16
USERS = 16384
ITEMS = 8192
IS = 256
FBS_U = 784
FBS_I = 392
N_FEAT = 2
N_ROWS = 16


def with_ends(result, rng, low, top_value):
    spot = [jax.random.randint(jax.random.fold_in(rng, axis), (), 0, length) for axis, length in enumerate(result.shape)]
    widest = result.shape.index(max(result.shape))
    neighbour = spot[:widest] + [(spot[widest] + 1) % result.shape[widest]] + spot[widest + 1:]
    return result.at[tuple(spot)].set(low).at[tuple(neighbour)].set(top_value)


def levels(rng, extent, split, smallest, largest):
    def one(position, shards_of):
        heights = jax.random.uniform(jax.random.fold_in(jax.random.fold_in(rng, 6), position), (shards_of,), jnp.float32, smallest / len(split), largest / len(split))
        return jnp.repeat(jnp.exp(heights), extent[position] // shards_of).reshape((-1,) + (1,) * (len(extent) - position - 1))

    loudness = one(*split[0])
    for cut in split[1:]:
        loudness = loudness * one(*cut)
    return loudness


def rank_table(amount, slope):
    portions = [(1 << 20) // math.isqrt(grade ** slope) + 1 for grade in range(1, amount + 1)]
    scale = 1 + sum(portions) // (1 << 30)
    return np.cumsum(np.array([max(1, weight // scale) for weight in portions]))


def ranked_ids(rng, shape, number_of, slope):
    listing = rank_table(number_of, slope)
    lot = jax.random.randint(jax.random.fold_in(rng, 1), shape, 0, int(listing[number_of - 1]))
    standing = jnp.searchsorted(jnp.asarray(listing, jnp.int32), lot, side="right")
    return jax.random.permutation(jax.random.fold_in(rng, 2), number_of)[standing].astype(jnp.int32)


def normal_values(rng, shape, scale, reach, pieces=(), kind=jnp.bfloat16):
    array = scale * jax.random.normal(rng, shape, jnp.float32)
    if pieces:
        array = array * levels(rng, shape, pieces, -0.22, 0.18)
    return jnp.clip(array, -reach, reach).astype(kind)


def setup_inputs(seed: int = 0) -> dict:
    arg_keys = jax.random.split(jax.random.key(seed), 9)
    return {
        "x_vals": normal_values(arg_keys[0], (NUB, N_FEAT, KBF, TILE, FBW), 1.0, 6.0, ((0, 16), (1, 2))),
        "x_blocks": with_ends(ranked_ids(arg_keys[1], (NUB, N_FEAT, KBF), FBS_U, 2), jax.random.fold_in(arg_keys[1], 3), 0, FBS_U - 1).astype(jnp.int32),
        "y_vals": normal_values(arg_keys[2], (NIB, N_FEAT, KBI, TILE, FBW), 1.0, 6.0, ((0, 16), (1, 2))),
        "y_blocks": with_ends(ranked_ids(arg_keys[3], (NIB, N_FEAT, KBI), FBS_I, 2), jax.random.fold_in(arg_keys[3], 3), 0, FBS_I - 1).astype(jnp.int32),
        "user_weights": normal_values(arg_keys[4], (RANK, FU), (KBF * N_FEAT * FBW) ** -0.5, 0.125, ((0, 16), (1, 2))),
        "item_weights": normal_values(arg_keys[5], (RANK, FI), (KBI * N_FEAT * FBW) ** -0.5, 0.125, ((0, 16), (1, 2))),
        "observed": with_ends((jax.random.randint(arg_keys[6], (NUB, NIB), 0, 2) < 1).astype(jnp.int32), jax.random.fold_in(arg_keys[6], 1), 0, 1),
        "ratings": normal_values(arg_keys[7], (USERS, N_FEAT, ITEMS // N_FEAT), 1.0, 6.0, ((0, 16), (1, 2))),
    }


def project(values, indices, weights_t, shard_blocks):
    blocks_table = weights_t.reshape(RANK, N_FEAT, shard_blocks, FBW)
    feat_index = jnp.arange(N_FEAT, dtype=jnp.int32)[:, None]

    def project_block(pair):
        block_values, block_indices = pair
        chosen = blocks_table[:, feat_index, block_indices.astype(jnp.int32)]
        return jnp.einsum('fktc,rfkc->tr', block_values.astype(jnp.float32), chosen.astype(jnp.float32))
    summed = lax.map(project_block, (values, indices))
    return summed.reshape(-1, RANK).astype(jnp.bfloat16)

def block_grads(values, indices, grads, shard_blocks):
    feat_index = jnp.arange(N_FEAT, dtype=jnp.int32)[:, None]
    totals = jnp.zeros((RANK, N_FEAT, shard_blocks, FBW), jnp.float32)

    def add_block(current, triple):
        block_values, block_indices, block_grads_now = triple
        contrib = jnp.einsum('tr,fktc->rfkc', block_grads_now.astype(jnp.float32), block_values.astype(jnp.float32))
        return (current.at[:, feat_index, block_indices.astype(jnp.int32)].add(contrib), None)
    totals, unused = lax.scan(add_block, totals, (values, indices, grads.reshape(-1, TILE, RANK)))
    return totals.reshape(RANK, -1)

def reference(x_vals, x_blocks, y_vals, y_blocks, user_weights, item_weights, observed, ratings):
    rank_scale = 1.0 / math.sqrt(RANK)
    grad_scale = 1.0 / (TILE * math.sqrt(RANK))
    user_proj = project(x_vals, x_blocks, user_weights, FBS_U)
    item_proj = project(y_vals, y_blocks, item_weights, FBS_I)

    def tile_step(item_total, triple):
        user_rows, rating_block, tile_row = triple
        rating_rows = rating_block.reshape(TILE, N_FEAT, N_ROWS, IS).transpose(0, 2, 1, 3).reshape(TILE, ITEMS)
        tile_mask = jnp.repeat(tile_row.astype(jnp.float32), TILE)
        predicted = jnp.dot(user_rows, item_proj.T, preferred_element_type=jnp.float32) * rank_scale
        residual = (tile_mask[None, :] * (predicted - rating_rows.astype(jnp.float32))).astype(jnp.bfloat16)
        user_grad_rows = (jnp.dot(residual, item_proj, preferred_element_type=jnp.float32) * grad_scale).astype(jnp.bfloat16)
        item_total = item_total + jnp.dot(residual.T, user_rows, preferred_element_type=jnp.float32)
        return (item_total, user_grad_rows)
    item_total = jnp.zeros((ITEMS, RANK), jnp.float32)
    item_total, user_grad_proj = lax.scan(tile_step, item_total, (user_proj.reshape(NUB, TILE, RANK), ratings.reshape(NUB, TILE, N_FEAT, N_ROWS * IS), observed))
    item_grad_proj = (item_total * grad_scale).astype(jnp.bfloat16)
    grad_user = block_grads(x_vals, x_blocks, user_grad_proj.reshape(-1, RANK), FBS_U)
    grad_item = block_grads(y_vals, y_blocks, item_grad_proj, FBS_I)
    return (grad_user, grad_item)
```

```python
import functools
import math

import jax
import jax.numpy as jnp
from jax import lax
from jax.experimental import pallas as pl
from jax.experimental.pallas import tpu as pltpu
from jax.sharding import PartitionSpec as P

FBW = 128
F32 = jnp.float32
BF16 = jnp.bfloat16
VMEM = pl.BlockSpec(memory_space=pltpu.VMEM)
SMEM = pl.BlockSpec(memory_space=pltpu.SMEM)


def params(mib):
    return pltpu.CompilerParams(vmem_limit_bytes=mib * 1024 * 1024)


def pick_kernel(ids, weights, out):
    peers, nb, _, width = out.shape
    kb = width // FBW

    def one(p, carry):
        for b in range(nb):
            for k in range(kb):
                at = pl.multiple_of(ids[(p * nb + b) * kb + k] * FBW, FBW)
                out[p, b, :, k * FBW : (k + 1) * FBW] = weights[:, pl.ds(at, FBW)]
        return carry

    lax.fori_loop(0, peers, one, 0)


def pick(ids, weights, peers, nb, kb):
    rp = weights.shape[0]
    return pl.pallas_call(
        pick_kernel,
        out_shape=jax.ShapeDtypeStruct((peers, nb, rp, kb * FBW), BF16),
        in_specs=[SMEM, VMEM],
        out_specs=VMEM,
        compiler_params=params(16),
        name="pick",
    )(ids, weights)


def joined(vals, b):
    return jnp.concatenate([vals[b, k] for k in range(vals.shape[1])], axis=1)


def project(vals, cols, b):
    peers, _, rp, width = cols.shape
    table = cols[:, b].reshape(peers * rp, width)
    return lax.dot_general(
        joined(vals, b), table, (((1,), (1,)), ((), ())), preferred_element_type=F32
    )


def user_proj_kernel(vals, cols, out):
    for b in range(vals.shape[0]):
        out[b] = project(vals, cols, b).astype(out.dtype)


def user_project(vals, cols):
    nb, _, tile, _ = vals.shape
    rank = cols.shape[0] * cols.shape[2]
    return pl.pallas_call(
        user_proj_kernel,
        out_shape=jax.ShapeDtypeStruct((nb, tile, rank), F32),
        in_specs=[VMEM, VMEM],
        out_specs=VMEM,
        compiler_params=params(24),
        name="user_project",
    )(vals, cols)


def grad_blocks_kernel(grads, vals, out):
    peers, nb, rp, width = out.shape
    for b in range(nb):
        blocks = lax.dot_general(
            grads[b], joined(vals, b), (((0,), (0,)), ((), ())), preferred_element_type=F32
        )
        out[:, b] = blocks.astype(out.dtype).reshape(peers, rp, width)


def grad_blocks(grads, vals, peers):
    nb, kb, tile, _ = vals.shape
    rank = grads.shape[-1]
    return pl.pallas_call(
        grad_blocks_kernel,
        out_shape=jax.ShapeDtypeStruct((peers, nb, rank // peers, kb * FBW), BF16),
        in_specs=[VMEM, VMEM],
        out_specs=VMEM,
        compiler_params=params(24),
        name="grad_blocks",
    )(grads, vals)


def gather_grads_kernel(ids, back, out):
    peers, nb, _, width = back.shape
    kb = width // FBW
    out[...] = jnp.zeros_like(out)

    def one(p, carry):
        for b in range(nb):
            for k in range(kb):
                at = pl.multiple_of(ids[(p * nb + b) * kb + k] * FBW, FBW)
                out[:, pl.ds(at, FBW)] += back[p, b, :, k * FBW : (k + 1) * FBW].astype(F32)
        return carry

    lax.fori_loop(0, peers, one, 0)


def gather_grads(ids, back, columns):
    return pl.pallas_call(
        gather_grads_kernel,
        out_shape=jax.ShapeDtypeStruct((back.shape[2], columns), F32),
        in_specs=[SMEM, VMEM],
        out_specs=VMEM,
        compiler_params=params(24),
        name="gather_grads",
    )(ids, back)


def rating_columns(ratings, row, tile, g, share):
    rows = pl.ds(row, tile)
    if share % FBW == 0:
        return ratings[rows, pl.ds(pl.multiple_of(g * share, share), share)]
    parts = FBW // share
    wide = ratings[rows, pl.ds(pl.multiple_of(g // parts * FBW, FBW), FBW)]
    picked = wide[:, :share]
    for part in range(1, parts):
        picked = jnp.where(g % parts == part, wide[:, part * share : (part + 1) * share], picked)
    return picked


def rating_kernel(
    rank_scale, grad_scale, me, observed, users, *refs
):
    peers = len(refs) - 5
    items, (ratings, grad, keep, give, total) = refs[:peers], refs[peers:]
    share = items[0].shape[0]
    nb, tile, rank = users.shape
    groups = observed.shape[0] // nb
    for b in range(nb):
        grad[b] = jnp.zeros((tile, rank), F32)
    for k in range(peers):
        g = lax.bitwise_xor(me[0], k)
        total[...] = jnp.zeros_like(total)

        def block(b, carry):
            @pl.when(observed[b * groups + g] != 0)
            def _():
                table = items[k][...]
                rows = users[b]
                predicted = lax.dot_general(
                    rows, table, (((1,), (1,)), ((), ())), preferred_element_type=F32
                )
                rated = rating_columns(ratings, pl.multiple_of(b * tile, tile), tile, g, share)
                residual = (predicted * rank_scale - rated.astype(F32)) * observed[
                    b * groups + g
                ].astype(F32)
                residual = residual.astype(BF16)
                grad[b] += jnp.dot(residual, table, preferred_element_type=F32) * grad_scale
                total[...] += lax.dot_general(
                    residual, rows, (((0,), (0,)), ((), ())), preferred_element_type=F32
                )

            return carry

        lax.fori_loop(0, nb, block, 0)
        (give if k % 2 else keep)[k // 2] = (total[...] * grad_scale).astype(BF16)


def rate(me, observed, users, items, ratings, rank_scale, grad_scale):
    peers = len(items)
    share, rank = items[0].shape
    half = jax.ShapeDtypeStruct((peers // 2, share, rank), BF16)
    return pl.pallas_call(
        functools.partial(rating_kernel, rank_scale, grad_scale),
        out_shape=(jax.ShapeDtypeStruct(users.shape, F32), half, half),
        in_specs=[SMEM, SMEM] + [VMEM] * (peers + 2),
        out_specs=(VMEM, VMEM, VMEM),
        scratch_shapes=[pltpu.VMEM((share, rank), F32)],
        compiler_params=params(40),
        name="rate",
    )(me, observed, users, *items, ratings)


def across(n, bit):
    return [(i, i ^ bit) for i in range(n)]


def on_device(n_feat, n_rows, x_vals, x_blocks, y_vals, y_blocks, user_weights, item_weights, observed, ratings):
    x_vals, y_vals = x_vals[:, 0], y_vals[:, 0]
    nb, kbu, tile, _ = x_vals.shape
    ni, kbi, _, _ = y_vals.shape
    rank = user_weights.shape[0] * n_rows
    rank_scale = 1.0 / math.sqrt(rank)
    grad_scale = 1.0 / (tile * math.sqrt(rank))
    share = ni * tile // n_feat
    feat_id = lax.axis_index("feat")
    row_id = lax.axis_index("rows")

    def swap(array):
        return lax.ppermute(array, "feat", across(2, 1))

    def every(array):
        return lax.all_to_all(array, "rows", split_axis=0, concat_axis=0, tiled=True)

    mine = jnp.concatenate([x_blocks.reshape(-1), y_blocks.reshape(-1)])
    ids = every(jnp.broadcast_to(mine, (n_rows, mine.shape[0])))
    user_ids = ids[:, : nb * kbu].reshape(-1)
    item_ids = ids[:, nb * kbu :].reshape(-1)

    item_cols = every(pick(item_ids, item_weights, n_rows, ni, kbi))
    item_part = user_project(y_vals, item_cols).reshape(ni * tile, rank)
    if n_feat == 2:
        own = lax.dynamic_slice_in_dim(item_part, feat_id * share, share, 0)
        other = lax.dynamic_slice_in_dim(item_part, (1 - feat_id) * share, share, 0)
        item_share = (own + swap(other.astype(BF16)).astype(F32)).astype(BF16)
    else:
        item_share = lax.psum_scatter(item_part, "feat", scatter_dimension=0, tiled=True).astype(BF16)

    items = {0: item_share}
    bit = n_rows // 2
    while bit:
        for k in list(items):
            items[k + bit] = lax.ppermute(items[k], "rows", across(n_rows, bit))
        bit //= 2
    items = [items[k] for k in range(n_rows)]

    user_cols = every(pick(user_ids, user_weights, n_rows, nb, kbu))
    user_part = user_project(x_vals, user_cols)
    if n_feat == 2:
        user_proj = (user_part + swap(user_part.astype(BF16)).astype(F32)).astype(BF16)
    else:
        user_proj = lax.psum(user_part, "feat").astype(BF16)

    grad_part, keep, give = rate(
        row_id.reshape(1).astype(jnp.int32),
        observed.reshape(-1),
        user_proj,
        items,
        ratings[:, 0],
        rank_scale,
        grad_scale,
    )
    if n_feat == 2:
        user_grad = (grad_part + swap(grad_part.astype(BF16)).astype(F32)).astype(BF16)
    else:
        user_grad = lax.psum(grad_part, "feat").astype(BF16)

    user_back = every(grad_blocks(user_grad, x_vals, n_rows))

    bit = 1
    while bit < n_rows:
        total = keep.astype(F32) + lax.ppermute(give, "rows", across(n_rows, bit)).astype(F32)
        total = total.astype(BF16)
        bit *= 2
        if bit < n_rows:
            pairs = total.reshape(-1, 2, share, rank)
            keep, give = pairs[:, 0], pairs[:, 1]
    item_grad = total[0]
    if n_feat == 2:
        other = swap(item_grad)
        first = feat_id == 0
        item_grad = jnp.concatenate(
            [jnp.where(first, item_grad, other), jnp.where(first, other, item_grad)]
        )
    else:
        item_grad = lax.all_gather(item_grad, "feat", axis=0, tiled=True)
    item_back = every(grad_blocks(item_grad.reshape(ni, tile, rank), y_vals, n_rows))

    return (
        gather_grads(user_ids, user_back, user_weights.shape[1]),
        gather_grads(item_ids, item_back, item_weights.shape[1]),
    )


def solution(mesh):
    return jax.shard_map(
        functools.partial(on_device, mesh.shape["feat"], mesh.shape["rows"]),
        mesh=mesh,
        in_specs=(
            P("rows", "feat", None, None, None),
            P("rows", "feat", None),
            P("rows", "feat", None, None, None),
            P("rows", "feat", None),
            P("rows", "feat"),
            P("rows", "feat"),
            P("rows", None),
            P("rows", "feat", None),
        ),
        out_specs=(P("rows", "feat"), P("rows", "feat")),
        check_vma=False,
    )
```

```python
import functools
import math

import jax
import jax.numpy as jnp
from jax import lax
from jax.experimental import pallas as pl
from jax.experimental.pallas import tpu as pltpu
from jax.sharding import PartitionSpec as P

FBW = 128
F32 = jnp.float32
BF16 = jnp.bfloat16
VMEM = pl.BlockSpec(memory_space=pltpu.VMEM)
SMEM = pl.BlockSpec(memory_space=pltpu.SMEM)
HBM = pl.BlockSpec(memory_space=pltpu.HBM)
ANY = pl.BlockSpec(memory_space=pl.ANY)


def params(mib):
    return pltpu.CompilerParams(vmem_limit_bytes=mib * 1024 * 1024)


def ask_kernel(x_blocks, y_blocks, out):
    rows = [x_blocks[b] for b in range(x_blocks.shape[0])]
    rows += [y_blocks[b] for b in range(y_blocks.shape[0])]
    used = sum(row.shape[1] for row in rows)
    rows.append(jnp.zeros((1, out.shape[2] - used), jnp.int32))
    out[...] = jnp.broadcast_to(jnp.concatenate(rows, axis=1)[None], out.shape)


def ask(x_blocks, y_blocks, peers):
    return pl.pallas_call(
        ask_kernel,
        out_shape=jax.ShapeDtypeStruct((peers, 1, FBW), jnp.int32),
        in_specs=[VMEM, VMEM],
        out_specs=VMEM,
        name="ask",
    )(x_blocks, y_blocks)


def preload_kernel(*refs):
    n = len(refs) // 2
    sems = refs[-1]
    copies = [
        pltpu.make_async_copy(refs[i], refs[n + i], sems.at[i]) for i in range(n)
    ]
    for copy in copies:
        copy.start()
    for copy in copies:
        copy.wait()


def preload(*arrays):
    return pl.pallas_call(
        preload_kernel,
        out_shape=[pltpu.VMEM(array.shape, array.dtype) for array in arrays],
        in_specs=[HBM] * len(arrays),
        out_specs=[VMEM] * len(arrays),
        scratch_shapes=[pltpu.SemaphoreType.DMA((len(arrays),))],
        compiler_params=params(12),
        name="preload",
    )(*[in_hbm(array) for array in arrays])


def pick_kernel(first, nb, ids, item_table, user_weights, out, user_table, sem, table_sem):
    peers, _, width = out.shape
    kb = width // FBW // (1 + nb)
    fetch_users = pltpu.make_async_copy(user_weights, user_table, table_sem)
    fetch_users.start()

    def picks(source, ids_at, to):
        def one(p, carry):
            for k in range(kb):
                at = pl.multiple_of(ids[p, 0, ids_at + k] * FBW, FBW)
                pltpu.make_async_copy(
                    source.at[:, pl.ds(at, FBW)], out.at[p, :, pl.ds((to + k) * FBW, FBW)], sem
                ).start()
            return carry

        lax.fori_loop(0, peers, one, 0)

    picks(item_table, first, 0)
    fetch_users.wait()
    for b in range(nb):
        picks(user_table, b * kb, (1 + b) * kb)
    pltpu.make_async_copy(out, out, sem).wait()


def pick(ids, item_table, user_weights, first, nb, kb):
    shape = (ids.shape[0], item_table.shape[0], (1 + nb) * kb * FBW)
    return pl.pallas_call(
        functools.partial(pick_kernel, first, nb),
        out_shape=pltpu.HBM(shape, BF16),
        in_specs=[SMEM, VMEM, HBM],
        out_specs=HBM,
        scratch_shapes=[
            pltpu.VMEM(user_weights.shape, BF16),
            pltpu.SemaphoreType.DMA,
            pltpu.SemaphoreType.DMA,
        ],
        compiler_params=params(8),
        name="pick",
    )(ids, item_table, in_hbm(user_weights))


def joined(vals):
    return jnp.concatenate([vals[k] for k in range(vals.shape[0])], axis=1)


def block_spec(vals, b):
    return pl.BlockSpec((1,) + vals.shape[1:], lambda i: (b, 0, 0, 0))


def part_spec(vals, cols, part):
    width = vals.shape[1] * FBW
    return pl.BlockSpec((cols.shape[0], cols.shape[1], width), lambda i: (0, 0, part))


def projected(vals, cols):
    peers, rp, width = cols.shape
    return lax.dot_general(
        joined(vals[0]),
        cols[...].reshape(peers * rp, width),
        (((1,), (1,)), ((), ())),
        preferred_element_type=F32,
    )


def project_kernel(vals, cols, *refs):
    own, send = refs[-2:]
    part = projected(vals, cols)
    own[...] = part
    send[...] = part.astype(BF16)


def project(vals, b, cols, part, follows=()):
    shape = (vals.shape[2], cols.shape[0] * cols.shape[1])
    return pl.pallas_call(
        project_kernel,
        out_shape=(jax.ShapeDtypeStruct(shape, F32), jax.ShapeDtypeStruct(shape, BF16)),
        grid=(1,),
        in_specs=[block_spec(vals, b), part_spec(vals, cols, part)]
        + [ANY] * len(follows),
        out_specs=(VMEM, VMEM),
        compiler_params=params(12),
        name="project",
    )(vals, cols, *follows)


def halves_kernel(feat, vals, cols, own, send):
    share = own.shape[0]
    part = projected(vals, cols)
    low, high = part[:share], part[share:]
    first = feat[0] == 0
    own[...] = jnp.where(first, low, high)
    send[...] = jnp.where(first, high, low).astype(BF16)


def project_halves(feat, vals, cols, part):
    share, rank = vals.shape[2] // 2, cols.shape[0] * cols.shape[1]
    return pl.pallas_call(
        halves_kernel,
        out_shape=(
            jax.ShapeDtypeStruct((share, rank), F32),
            jax.ShapeDtypeStruct((share, rank), BF16),
        ),
        grid=(1,),
        in_specs=[SMEM, block_spec(vals, 0), part_spec(vals, cols, part)],
        out_specs=(VMEM, VMEM),
        compiler_params=params(12),
        name="project_halves",
    )(feat, vals, cols)


def user_grad_kernel(vals, *refs):
    grads, out = refs[: 2 * vals.shape[0]], refs[-1]
    peers, rp, _ = out.shape
    kb = vals.shape[1]
    for b in range(vals.shape[0]):
        own, other = grads[2 * b], grads[2 * b + 1]
        grad = (own[...] + other[...].astype(F32)).astype(BF16)
        blocks = lax.dot_general(
            grad, joined(vals[b]), (((0,), (0,)), ((), ())), preferred_element_type=F32
        )
        out[:, :, b * kb * FBW : (b + 1) * kb * FBW] = blocks.astype(out.dtype).reshape(
            peers, rp, kb * FBW
        )


def user_grad_blocks(grads, vals, peers, follows):
    nb, kb, _, _ = vals.shape
    rank = grads[0].shape[1]
    shape = (peers, rank // peers, nb * kb * FBW)
    return pl.pallas_call(
        user_grad_kernel,
        out_shape=pltpu.HBM(shape, BF16),
        grid=(1,),
        in_specs=[VMEM] * (1 + len(grads)) + [ANY] * len(follows),
        out_specs=pl.BlockSpec(shape, lambda i: (0, 0, 0)),
        compiler_params=params(16),
        name="user_grad_blocks",
    )(vals, *grads, *follows)


def item_grad_kernel(grads, vals, follows, out):
    peers, rp, width = out.shape
    blocks = jnp.dot(grads[...], joined(vals[0]), preferred_element_type=F32)
    out[...] = blocks.astype(out.dtype).reshape(peers, rp, width)


def item_grad_blocks(grads, vals, b, peers, follows):
    _, kb, _, _ = vals.shape
    shape = (peers, grads.shape[0] // peers, kb * FBW)
    return pl.pallas_call(
        item_grad_kernel,
        out_shape=pltpu.HBM(shape, BF16),
        in_specs=[VMEM, block_spec(vals, b), ANY],
        out_specs=pl.BlockSpec(shape, lambda i: (0, 0, 0)),
        grid=(1,),
        compiler_params=params(12),
        name="item_grad_blocks",
    )(grads, vals, follows)


def collect_kernel(first, ids, back, out):
    peers, _, width = back.shape
    out[...] = jnp.zeros_like(out)

    def one(p, carry):
        for k in range(width // FBW):
            at = pl.multiple_of(ids[p, 0, first + k] * FBW, FBW)
            out[:, pl.ds(at, FBW)] += back[p, :, k * FBW : (k + 1) * FBW].astype(F32)
        return carry

    lax.fori_loop(0, peers, one, 0)


def collect(ids, back, first, columns):
    return pl.pallas_call(
        functools.partial(collect_kernel, first),
        out_shape=jax.ShapeDtypeStruct((back.shape[1], columns), F32),
        in_specs=[SMEM, VMEM],
        out_specs=VMEM,
        compiler_params=params(12),
        name="collect",
    )(ids, back)


def rating_columns(rated, g, share):
    if share % FBW == 0:
        return rated
    parts = FBW // share
    picked = rated[:, :share]
    for part in range(1, parts):
        picked = jnp.where(g % parts == part, rated[:, part * share : (part + 1) * share], picked)
    return picked


def place(k, bits):
    index = 0
    for bit in bits:
        index = 2 * index + (k & bit != 0)
    return k & 1, index


def rating_kernel(orders, rank_scale, grad_scale, me, observed, *refs):
    peers = 2 << len(orders[0])
    nb = observed.shape[0]
    parts, refs = refs[: 2 * nb], refs[2 * nb :]
    items, ratings, refs = refs[:peers], refs[peers], refs[peers + 1 :]
    grads, totals, refs = refs[: 2 * nb], refs[2 * nb : 2 * nb + 4], refs[2 * nb + 4 :]
    rated, table, sems, users, users_t, residuals = refs
    share = items[0].shape[0]
    tile, rank = parts[0].shape
    wide = rated.shape[2]
    width = 4

    def fetch(k):
        g = lax.bitwise_xor(me[0], k)
        at = pl.multiple_of(g * share // wide * wide, wide)
        return (
            pltpu.make_async_copy(ratings.at[:, pl.ds(at, wide)], rated.at[k], sems.at[0, k]),
            pltpu.make_async_copy(items[k], table.at[pl.ds(k * share, share), :], sems.at[1, k]),
        )

    for k in range(peers):
        for copy in fetch(k):
            copy.start()
    for b in range(nb):
        own, other = parts[2 * b], parts[2 * b + 1]
        rows = (own[...] + other[...].astype(F32)).astype(BF16)
        users[b * tile : (b + 1) * tile, :] = rows
        users_t[:, b * tile : (b + 1) * tile] = rows.T
    for k in range(peers):
        g = lax.bitwise_xor(me[0], k)
        columns = pl.ds(k * share, share)
        for copy in fetch(k):
            copy.wait()
        for b in range(nb):
            rows = slice(b * tile, (b + 1) * tile)
            seen = observed[b, g]

            @pl.when(seen != 0)
            def _():
                predicted = lax.dot_general(
                    users[rows, :],
                    table[columns, :],
                    (((1,), (1,)), ((), ())),
                    preferred_element_type=F32,
                )
                rating = rating_columns(rated[k, rows, :], g, share).astype(F32)
                residual = (predicted * rank_scale - rating) * seen.astype(F32)
                residuals[rows, columns] = residual.astype(BF16)

            @pl.when(seen == 0)
            def _():
                residuals[rows, columns] = jnp.zeros((tile, share), BF16)

        if k % width == width - 1:
            start = k - width + 1
            terms = jnp.dot(
                users_t[...],
                residuals[:, pl.ds(start * share, width * share)],
                preferred_element_type=F32,
            )
            for j in range(width):
                term = terms[:, j * share : (j + 1) * share] * grad_scale
                for h, order in enumerate(orders):
                    group, index = place(start + j, order)
                    part = term[h * rank // 2 : (h + 1) * rank // 2]
                    totals[2 * h + group][index] = part.astype(BF16)
    step = tile // 4
    for b in range(nb):
        grad, grad_send = grads[2 * b], grads[2 * b + 1]
        for r in range(0, tile, step):
            part = jnp.dot(
                residuals[b * tile + r : b * tile + r + step, :],
                table[...],
                preferred_element_type=F32,
            )
            part = part * grad_scale
            grad[r : r + step, :] = part
            grad_send[r : r + step, :] = part.astype(BF16)


def in_hbm(array):
    return pltpu.with_memory_space_constraint(array, pltpu.HBM)


def rate(orders, me, observed, parts, items, ratings, rank_scale, grad_scale):
    peers = len(items)
    share, rank = items[0].shape
    nb = observed.shape[0]
    tile = parts[0].shape[0]
    quarter = jax.ShapeDtypeStruct((peers // 2, rank // 2, share), BF16)
    outs = [jax.ShapeDtypeStruct((tile, rank), F32), jax.ShapeDtypeStruct((tile, rank), BF16)]
    outs = outs * nb + [quarter] * 4
    return pl.pallas_call(
        functools.partial(rating_kernel, orders, rank_scale, grad_scale),
        out_shape=outs,
        in_specs=[SMEM, SMEM] + [VMEM] * (2 * nb) + [ANY] * peers + [HBM],
        out_specs=[VMEM] * len(outs),
        scratch_shapes=[
            pltpu.VMEM((peers, nb * tile, max(share, FBW)), BF16),
            pltpu.VMEM((peers * share, rank), BF16),
            pltpu.SemaphoreType.DMA((2, peers)),
            pltpu.VMEM((nb * tile, rank), BF16),
            pltpu.VMEM((rank, nb * tile), BF16),
            pltpu.VMEM((nb * tile, peers * share), BF16),
        ],
        compiler_params=params(36),
        name="rate",
    )(me, observed, *parts, *items, in_hbm(ratings))


def after_kernel(*refs):
    pass


def after(arrays, follows):
    n = len(arrays)
    return pl.pallas_call(
        after_kernel,
        out_shape=[jax.ShapeDtypeStruct(array.shape, array.dtype) for array in arrays],
        in_specs=[ANY] * (n + len(follows)),
        out_specs=[ANY] * n,
        input_output_aliases={i: i for i in range(n)},
        name="after",
    )(*arrays, *follows)


def across(n, bit):
    return [(i, i ^ bit) for i in range(n)]


def on_device(n_feat, n_rows, x_vals, x_blocks, y_vals, y_blocks, user_weights, item_weights, observed, ratings):
    x_vals, y_vals = x_vals[:, 0], y_vals[:, 0]
    nb, kbu, tile, _ = x_vals.shape
    ni, kbi, _, _ = y_vals.shape
    rank = user_weights.shape[0] * n_rows
    rank_scale = 1.0 / math.sqrt(rank)
    grad_scale = 1.0 / (tile * math.sqrt(rank))
    share = ni * tile // n_feat
    feat_id = lax.axis_index("feat")
    row_id = lax.axis_index("rows")

    def swap(array):
        return lax.ppermute(array, "feat", across(2, 1))

    def every(array):
        return lax.all_to_all(array, "rows", split_axis=0, concat_axis=0, tiled=True)

    def feat_sum(own, send):
        if n_feat == 2:
            return own, swap(send)
        return lax.psum(own, "feat"), jnp.zeros_like(send)

    ids = every(ask(x_blocks, y_blocks, n_rows))
    (item_table,) = preload(item_weights)
    cols = every(pick(ids, item_table, user_weights, nb * kbu, nb, kbu))
    if n_feat == 2:
        feat = feat_id.reshape(1).astype(jnp.int32)
        own, send = project_halves(feat, y_vals, cols, 0)
        item_share = (own + swap(send).astype(F32)).astype(BF16)
    else:
        own, send = project(y_vals, 0, cols, 0)
        item_share = lax.psum_scatter(own, "feat", scatter_dimension=0, tiled=True).astype(BF16)
    parts = []
    for b in range(nb):
        parts.extend(feat_sum(*project(x_vals, b, cols, 1 + b, (send,))))

    items = {0: item_share}
    bit = n_rows // 2
    while bit:
        for k in list(items):
            items[k + bit] = lax.ppermute(items[k], "rows", across(n_rows, bit))
        bit //= 2
    items = [items[k] for k in range(n_rows)]

    me = row_id.reshape(1).astype(jnp.int32)
    bits = [1 << i for i in range(1, n_rows.bit_length() - 1)]
    orders = [bits, bits[1:] + bits[:1]]
    *grads, first, first_give, second, second_give = rate(
        orders, me, observed, parts, items, ratings[:, 0], rank_scale, grad_scale
    )
    grads = [part for b in range(nb) for part in feat_sum(*grads[2 * b : 2 * b + 2])]

    def plus(a, b):
        return (a.astype(F32) + b.astype(F32)).astype(BF16)

    def give(array, bit):
        return lax.ppermute(array, "rows", across(n_rows, bit))

    sums = [plus(first, give(first_give, 1)), plus(second, give(second_give, 1))]
    for step in range(len(bits)):
        for h, order in enumerate(orders):
            half = sums[h].shape[0] // 2
            sums[h] = plus(sums[h][:half], give(sums[h][half:], order[step]))
        if step == len(bits) - 2:
            user_ask = user_grad_blocks(grads, x_vals, n_rows, sums)
    item_grad = jnp.concatenate([part[0] for part in sums])
    user_back = every(*after([user_ask], [item_grad]))
    if n_feat == 2:
        other = swap(item_grad)
        first = feat_id == 0
        item_grad = jnp.concatenate(
            [jnp.where(first, item_grad, other), jnp.where(first, other, item_grad)], axis=1
        )
    else:
        item_grad = lax.all_gather(item_grad, "feat", axis=1, tiled=True)
    item_back = every(item_grad_blocks(item_grad, y_vals, 0, n_rows, user_back))

    return (
        collect(ids, user_back, 0, user_weights.shape[1]),
        collect(ids, item_back, nb * kbu, item_weights.shape[1]),
    )


def solution(mesh):
    return jax.shard_map(
        functools.partial(on_device, mesh.shape["feat"], mesh.shape["rows"]),
        mesh=mesh,
        in_specs=(
            P("rows", "feat", None, None, None),
            P("rows", "feat", None),
            P("rows", "feat", None, None, None),
            P("rows", "feat", None),
            P("rows", "feat"),
            P("rows", "feat"),
            P("rows", None),
            P("rows", "feat", None),
        ),
        out_specs=(P("rows", "feat"), P("rows", "feat")),
        check_vma=False,
    )
```

```python
import functools
import math

import jax
import jax.numpy as jnp
from jax import lax
from jax.experimental import pallas as pl
from jax.experimental.pallas import tpu as pltpu
from jax.sharding import PartitionSpec as P

FBW = 128
F32 = jnp.float32
BF16 = jnp.bfloat16
VMEM = pl.BlockSpec(memory_space=pltpu.VMEM)
SMEM = pl.BlockSpec(memory_space=pltpu.SMEM)
HBM = pl.BlockSpec(memory_space=pltpu.HBM)
ANY = pl.BlockSpec(memory_space=pl.ANY)


def params(mib):
    return pltpu.CompilerParams(vmem_limit_bytes=mib * 1024 * 1024)


def ask_kernel(x_blocks, y_blocks, out):
    rows = [x_blocks[b] for b in range(x_blocks.shape[0])]
    rows += [y_blocks[b] for b in range(y_blocks.shape[0])]
    used = sum(row.shape[1] for row in rows)
    rows.append(jnp.zeros((1, out.shape[2] - used), jnp.int32))
    out[...] = jnp.broadcast_to(jnp.concatenate(rows, axis=1)[None], out.shape)


def ask(x_blocks, y_blocks, peers):
    return pl.pallas_call(
        ask_kernel,
        out_shape=jax.ShapeDtypeStruct((peers, 1, FBW), jnp.int32),
        in_specs=[VMEM, VMEM],
        out_specs=VMEM,
        name="ask",
    )(x_blocks, y_blocks)


def preload_kernel(*refs):
    n = len(refs) // 2
    sems = refs[-1]
    copies = [
        pltpu.make_async_copy(refs[i], refs[n + i], sems.at[i]) for i in range(n)
    ]
    for copy in copies:
        copy.start()
    for copy in copies:
        copy.wait()


def preload(*arrays):
    return pl.pallas_call(
        preload_kernel,
        out_shape=[pltpu.VMEM(array.shape, array.dtype) for array in arrays],
        in_specs=[HBM] * len(arrays),
        out_specs=[VMEM] * len(arrays),
        scratch_shapes=[pltpu.SemaphoreType.DMA((len(arrays),))],
        compiler_params=params(12),
        name="preload",
    )(*[in_hbm(array) for array in arrays])


def pick_kernel(first, nb, ids, item_table, user_weights, out, user_table, message, sem, table_sem):
    peers, _, width = out.shape
    kb = width // FBW // (1 + nb)
    fetch_users = pltpu.make_async_copy(user_weights, user_table, table_sem)
    fetch_users.start()

    def pick_one(p, source, ids_at, to):
        at = pl.multiple_of(ids[p, 0, ids_at] * FBW, FBW)
        message[p, :, to * FBW : (to + 1) * FBW] = source[:, pl.ds(at, FBW)]

    def item_blocks(p, carry):
        for k in range(kb):
            pick_one(p, item_table, first + k, k)
        return carry

    def user_blocks(p, carry):
        for k in range(nb * kb):
            pick_one(p, user_table, k, kb + k)
        pltpu.make_async_copy(message.at[p], out.at[p], sem).start()
        return carry

    lax.fori_loop(0, peers, item_blocks, 0)
    fetch_users.wait()
    lax.fori_loop(0, peers, user_blocks, 0)
    pltpu.make_async_copy(message, out, sem).wait()


def pick(ids, item_table, user_weights, first, nb, kb):
    shape = (ids.shape[0], item_table.shape[0], (1 + nb) * kb * FBW)
    return pl.pallas_call(
        functools.partial(pick_kernel, first, nb),
        out_shape=pltpu.HBM(shape, BF16),
        in_specs=[SMEM, VMEM, HBM],
        out_specs=HBM,
        scratch_shapes=[
            pltpu.VMEM(user_weights.shape, BF16),
            pltpu.VMEM(shape, BF16),
            pltpu.SemaphoreType.DMA,
            pltpu.SemaphoreType.DMA,
        ],
        compiler_params=params(10),
        name="pick",
    )(ids, item_table, in_hbm(user_weights))


def joined(vals):
    return jnp.concatenate([vals[k] for k in range(vals.shape[0])], axis=1)


def block_spec(vals, b):
    return pl.BlockSpec((1,) + vals.shape[1:], lambda i: (b, 0, 0, 0))


def part_spec(vals, cols, part):
    width = vals.shape[1] * FBW
    return pl.BlockSpec((cols.shape[0], cols.shape[1], width), lambda i: (0, 0, part))


def projected(vals, cols):
    peers, rp, width = cols.shape
    return lax.dot_general(
        joined(vals[0]),
        cols[...].reshape(peers * rp, width),
        (((1,), (1,)), ((), ())),
        preferred_element_type=F32,
    )


def project_kernel(vals, cols, *refs):
    own, send = refs[-2:]
    part = projected(vals, cols)
    own[...] = part
    send[...] = part.astype(BF16)


def project(vals, b, cols, part, follows=()):
    shape = (vals.shape[2], cols.shape[0] * cols.shape[1])
    return pl.pallas_call(
        project_kernel,
        out_shape=(jax.ShapeDtypeStruct(shape, F32), jax.ShapeDtypeStruct(shape, BF16)),
        grid=(1,),
        in_specs=[block_spec(vals, b), part_spec(vals, cols, part)]
        + [ANY] * len(follows),
        out_specs=(VMEM, VMEM),
        compiler_params=params(12),
        name="project",
    )(vals, cols, *follows)


def halves_kernel(feat, vals, cols, own, send):
    share = own.shape[0]
    part = projected(vals, cols)
    low, high = part[:share], part[share:]
    first = feat[0] == 0
    own[...] = jnp.where(first, low, high)
    send[...] = jnp.where(first, high, low).astype(BF16)


def project_halves(feat, vals, cols, part):
    share, rank = vals.shape[2] // 2, cols.shape[0] * cols.shape[1]
    return pl.pallas_call(
        halves_kernel,
        out_shape=(
            jax.ShapeDtypeStruct((share, rank), F32),
            jax.ShapeDtypeStruct((share, rank), BF16),
        ),
        grid=(1,),
        in_specs=[SMEM, block_spec(vals, 0), part_spec(vals, cols, part)],
        out_specs=(VMEM, VMEM),
        compiler_params=params(12),
        name="project_halves",
    )(feat, vals, cols)


def user_grad_kernel(vals, *refs):
    grads, out = refs[: 2 * vals.shape[0]], refs[-1]
    peers, rp, _ = out.shape
    kb = vals.shape[1]
    for b in range(vals.shape[0]):
        own, other = grads[2 * b], grads[2 * b + 1]
        grad = (own[...] + other[...].astype(F32)).astype(BF16)
        blocks = lax.dot_general(
            grad, joined(vals[b]), (((0,), (0,)), ((), ())), preferred_element_type=F32
        )
        out[:, :, b * kb * FBW : (b + 1) * kb * FBW] = blocks.astype(out.dtype).reshape(
            peers, rp, kb * FBW
        )


def user_grad_blocks(grads, vals, peers, follows):
    nb, kb, _, _ = vals.shape
    rank = grads[0].shape[1]
    shape = (peers, rank // peers, nb * kb * FBW)
    return pl.pallas_call(
        user_grad_kernel,
        out_shape=pltpu.HBM(shape, BF16),
        grid=(1,),
        in_specs=[VMEM] * (1 + len(grads)) + [ANY] * len(follows),
        out_specs=pl.BlockSpec(shape, lambda i: (0, 0, 0)),
        compiler_params=params(16),
        name="user_grad_blocks",
    )(vals, *grads, *follows)


def item_grad_kernel(grads, vals, out):
    peers, rp, width = out.shape
    blocks = jnp.dot(grads[...], joined(vals[0]), preferred_element_type=F32)
    out[...] = blocks.astype(out.dtype).reshape(peers, rp, width)


def item_grad_blocks(grads, vals, b, peers):
    _, kb, _, _ = vals.shape
    shape = (peers, grads.shape[0] // peers, kb * FBW)
    return pl.pallas_call(
        item_grad_kernel,
        out_shape=pltpu.HBM(shape, BF16),
        in_specs=[VMEM, block_spec(vals, b)],
        out_specs=pl.BlockSpec(shape, lambda i: (0, 0, 0)),
        grid=(1,),
        compiler_params=params(12),
        name="item_grad_blocks",
    )(grads, vals)


def collect_kernel(first, ids, back, out):
    peers, _, width = back.shape
    out[...] = jnp.zeros_like(out)

    def one(p, carry):
        for k in range(width // FBW):
            at = pl.multiple_of(ids[p, 0, first + k] * FBW, FBW)
            out[:, pl.ds(at, FBW)] += back[p, :, k * FBW : (k + 1) * FBW].astype(F32)
        return carry

    lax.fori_loop(0, peers, one, 0)


def collect(ids, back, first, columns):
    return pl.pallas_call(
        functools.partial(collect_kernel, first),
        out_shape=jax.ShapeDtypeStruct((back.shape[1], columns), F32),
        grid=(1,),
        in_specs=[SMEM, pl.BlockSpec(back.shape, lambda i: (0, 0, 0))],
        out_specs=VMEM,
        compiler_params=params(16),
        name="collect",
    )(ids, back)


def rating_columns(rated, g, share):
    if share % FBW == 0:
        return rated
    parts = FBW // share
    picked = rated[:, :share]
    for part in range(1, parts):
        picked = jnp.where(g % parts == part, rated[:, part * share : (part + 1) * share], picked)
    return picked


def place(k, bits):
    index = 0
    for bit in bits:
        index = 2 * index + (k & bit != 0)
    return k & 1, index


def rating_kernel(orders, rank_scale, grad_scale, me, observed, *refs):
    peers = 2 << len(orders[0])
    nb = observed.shape[0]
    parts, refs = refs[: 2 * nb], refs[2 * nb :]
    items, ratings, refs = refs[:peers], refs[peers], refs[peers + 1 :]
    grads, totals, refs = refs[: 2 * nb], refs[2 * nb : 2 * nb + 4], refs[2 * nb + 4 :]
    rated, table, sems, users, users_t, residuals = refs
    share = items[0].shape[0]
    tile, rank = parts[0].shape
    wide = rated.shape[2]
    width = 8

    def fetch(k):
        g = lax.bitwise_xor(me[0], k)
        at = pl.multiple_of(g * share // wide * wide, wide)
        return (
            pltpu.make_async_copy(ratings.at[:, pl.ds(at, wide)], rated.at[k], sems.at[0, k]),
            pltpu.make_async_copy(items[k], table.at[pl.ds(k * share, share), :], sems.at[1, k]),
        )

    for k in range(peers):
        for copy in fetch(k):
            copy.start()
    for b in range(nb):
        own, other = parts[2 * b], parts[2 * b + 1]
        rows = (own[...] + other[...].astype(F32)).astype(BF16)
        users[b * tile : (b + 1) * tile, :] = rows
        users_t[:, b * tile : (b + 1) * tile] = rows.T
    residuals[...] = jnp.zeros_like(residuals)
    for k in range(peers):
        g = lax.bitwise_xor(me[0], k)
        columns = pl.ds(k * share, share)
        for copy in fetch(k):
            copy.wait()
        def tiles(rows):
            predicted = lax.dot_general(
                users[rows, :], table[columns, :], (((1,), (1,)), ((), ())), preferred_element_type=F32
            )
            rating = rating_columns(rated[k, rows, :], g, share).astype(F32)
            residuals[rows, columns] = (predicted * rank_scale - rating).astype(BF16)

        seen = [observed[b, g] != 0 for b in range(nb)]
        all_seen = functools.reduce(jnp.logical_and, seen)
        pl.when(all_seen)(functools.partial(tiles, slice(0, nb * tile)))
        for b in range(nb):
            alone = jnp.logical_and(seen[b], jnp.logical_not(all_seen))
            pl.when(alone)(functools.partial(tiles, slice(b * tile, (b + 1) * tile)))

        if k % width == width - 1:
            start = k - width + 1
            terms = jnp.dot(
                users_t[...],
                residuals[:, pl.ds(start * share, width * share)],
                preferred_element_type=F32,
            )
            for j in range(width):
                term = terms[:, j * share : (j + 1) * share] * grad_scale
                for h, order in enumerate(orders):
                    group, index = place(start + j, order)
                    part = term[h * rank // 2 : (h + 1) * rank // 2]
                    totals[2 * h + group][index] = part.astype(BF16)
    step = tile // 4
    for b in range(nb):
        grad, grad_send = grads[2 * b], grads[2 * b + 1]
        for r in range(0, tile, step):
            part = jnp.dot(
                residuals[b * tile + r : b * tile + r + step, :],
                table[...],
                preferred_element_type=F32,
            )
            part = part * grad_scale
            grad[r : r + step, :] = part
            grad_send[r : r + step, :] = part.astype(BF16)


def in_hbm(array):
    return pltpu.with_memory_space_constraint(array, pltpu.HBM)


def rate(orders, me, observed, parts, items, ratings, rank_scale, grad_scale):
    peers = len(items)
    share, rank = items[0].shape
    nb = observed.shape[0]
    tile = parts[0].shape[0]
    quarter = jax.ShapeDtypeStruct((peers // 2, rank // 2, share), BF16)
    outs = [jax.ShapeDtypeStruct((tile, rank), F32), jax.ShapeDtypeStruct((tile, rank), BF16)]
    outs = outs * nb + [quarter] * 4
    return pl.pallas_call(
        functools.partial(rating_kernel, orders, rank_scale, grad_scale),
        out_shape=outs,
        in_specs=[SMEM, SMEM] + [VMEM] * (2 * nb) + [ANY] * peers + [HBM],
        out_specs=[VMEM] * len(outs),
        scratch_shapes=[
            pltpu.VMEM((peers, nb * tile, max(share, FBW)), BF16),
            pltpu.VMEM((peers * share, rank), BF16),
            pltpu.SemaphoreType.DMA((2, peers)),
            pltpu.VMEM((nb * tile, rank), BF16),
            pltpu.VMEM((rank, nb * tile), BF16),
            pltpu.VMEM((nb * tile, peers * share), BF16),
        ],
        compiler_params=params(36),
        name="rate",
    )(me, observed, *parts, *items, in_hbm(ratings))


def after_kernel(*refs):
    pass


def after(arrays, follows):
    n = len(arrays)
    return pl.pallas_call(
        after_kernel,
        out_shape=[pltpu.HBM(array.shape, array.dtype) for array in arrays],
        in_specs=[HBM] * n + [ANY] * len(follows),
        out_specs=[HBM] * n,
        input_output_aliases={i: i for i in range(n)},
        name="after",
    )(*map(in_hbm, arrays), *follows)


def across(n, bit):
    return [(i, i ^ bit) for i in range(n)]


def on_device(n_feat, n_rows, x_vals, x_blocks, y_vals, y_blocks, user_weights, item_weights, observed, ratings):
    x_vals, y_vals = x_vals[:, 0], y_vals[:, 0]
    nb, kbu, tile, _ = x_vals.shape
    ni, kbi, _, _ = y_vals.shape
    rank = user_weights.shape[0] * n_rows
    rank_scale = 1.0 / math.sqrt(rank)
    grad_scale = 1.0 / (tile * math.sqrt(rank))
    share = ni * tile // n_feat
    feat_id = lax.axis_index("feat")
    row_id = lax.axis_index("rows")

    def swap(array):
        return lax.ppermute(array, "feat", across(2, 1))

    def every(array):
        return lax.all_to_all(array, "rows", split_axis=0, concat_axis=0, tiled=True)

    def feat_sum(own, send):
        if n_feat == 2:
            return own, swap(send)
        return lax.psum(own, "feat"), jnp.zeros_like(send)

    ids = every(ask(x_blocks, y_blocks, n_rows))
    (item_table,) = preload(item_weights)
    cols = every(pick(ids, item_table, user_weights, nb * kbu, nb, kbu))
    if n_feat == 2:
        feat = feat_id.reshape(1).astype(jnp.int32)
        own, send = project_halves(feat, y_vals, cols, 0)
        item_share = (own + swap(send).astype(F32)).astype(BF16)
    else:
        own, send = project(y_vals, 0, cols, 0)
        item_share = lax.psum_scatter(own, "feat", scatter_dimension=0, tiled=True).astype(BF16)
    parts = []
    for b in range(nb):
        parts.extend(feat_sum(*project(x_vals, b, cols, 1 + b, (send,))))

    items = {0: item_share}
    bit = n_rows // 2
    while bit:
        for k in list(items):
            items[k + bit] = lax.ppermute(items[k], "rows", across(n_rows, bit))
        bit //= 2
    items = [items[k] for k in range(n_rows)]

    me = row_id.reshape(1).astype(jnp.int32)
    bits = [1 << i for i in range(1, n_rows.bit_length() - 1)]
    orders = [bits, bits[1:] + bits[:1]]
    *grads, first, first_give, second, second_give = rate(
        orders, me, observed, parts, items, ratings[:, 0], rank_scale, grad_scale
    )
    grads = [part for b in range(nb) for part in feat_sum(*grads[2 * b : 2 * b + 2])]

    def plus(a, b):
        return (a.astype(F32) + b.astype(F32)).astype(BF16)

    def give(array, bit):
        return lax.ppermute(array, "rows", across(n_rows, bit))

    sums = [plus(first, give(first_give, 1)), plus(second, give(second_give, 1))]
    for step in range(len(bits)):
        for h, order in enumerate(orders):
            half = sums[h].shape[0] // 2
            sums[h] = plus(sums[h][:half], give(sums[h][half:], order[step]))
        if step == len(bits) - 2:
            user_ask = user_grad_blocks(grads, x_vals, n_rows, sums)
    item_grad = jnp.concatenate([part[0] for part in sums])
    user_back = in_hbm(every(*after([user_ask], sums)))
    if n_feat == 2:
        other = swap(item_grad)
        first = feat_id == 0
        item_grad = jnp.concatenate(
            [jnp.where(first, item_grad, other), jnp.where(first, other, item_grad)], axis=1
        )
    else:
        item_grad = lax.all_gather(item_grad, "feat", axis=1, tiled=True)
    item_back = every(*after([item_grad_blocks(item_grad, y_vals, 0, n_rows)], [user_back]))

    return (
        collect(ids, user_back, 0, user_weights.shape[1]),
        collect(ids, item_back, nb * kbu, item_weights.shape[1]),
    )


def solution(mesh):
    return jax.shard_map(
        functools.partial(on_device, mesh.shape["feat"], mesh.shape["rows"]),
        mesh=mesh,
        in_specs=(
            P("rows", "feat", None, None, None),
            P("rows", "feat", None),
            P("rows", "feat", None, None, None),
            P("rows", "feat", None),
            P("rows", "feat"),
            P("rows", "feat"),
            P("rows", None),
            P("rows", "feat", None),
        ),
        out_specs=(P("rows", "feat"), P("rows", "feat")),
        check_vma=False,
    )
```

```python
import functools
import math

import jax
import jax.numpy as jnp
from jax import lax
from jax.experimental import pallas as pl
from jax.experimental.pallas import tpu as pltpu
from jax.sharding import PartitionSpec as P

FBW = 128
F32 = jnp.float32
BF16 = jnp.bfloat16
VMEM = pl.BlockSpec(memory_space=pltpu.VMEM)
SMEM = pl.BlockSpec(memory_space=pltpu.SMEM)
HBM = pl.BlockSpec(memory_space=pltpu.HBM)
ANY = pl.BlockSpec(memory_space=pl.ANY)


def params(mib):
    return pltpu.CompilerParams(vmem_limit_bytes=mib * 1024 * 1024)


def ask_kernel(x_blocks, y_blocks, out):
    rows = [x_blocks[b] for b in range(x_blocks.shape[0])]
    rows += [y_blocks[b] for b in range(y_blocks.shape[0])]
    used = sum(row.shape[1] for row in rows)
    rows.append(jnp.zeros((1, out.shape[2] - used), jnp.int32))
    out[...] = jnp.broadcast_to(jnp.concatenate(rows, axis=1)[None], out.shape)


def ask(x_blocks, y_blocks, peers):
    return pl.pallas_call(
        ask_kernel,
        out_shape=jax.ShapeDtypeStruct((peers, 1, FBW), jnp.int32),
        in_specs=[VMEM, VMEM],
        out_specs=VMEM,
        name="ask",
    )(x_blocks, y_blocks)


def preload_kernel(*refs):
    n = len(refs) // 2
    sems = refs[-1]
    copies = [
        pltpu.make_async_copy(refs[i], refs[n + i], sems.at[i]) for i in range(n)
    ]
    for copy in copies:
        copy.start()
    for copy in copies:
        copy.wait()


def preload(*arrays):
    return pl.pallas_call(
        preload_kernel,
        out_shape=[pltpu.VMEM(array.shape, array.dtype) for array in arrays],
        in_specs=[HBM] * len(arrays),
        out_specs=[VMEM] * len(arrays),
        scratch_shapes=[pltpu.SemaphoreType.DMA((len(arrays),))],
        compiler_params=params(12),
        name="preload",
    )(*[in_hbm(array) for array in arrays])


def pick_kernel(first, nb, ids, item_table, user_weights, out, user_table, message, sem, table_sem):
    peers, _, width = out.shape
    kb = width // FBW // (1 + nb)
    fetch_users = pltpu.make_async_copy(user_weights, user_table, table_sem)
    fetch_users.start()

    def pick_one(p, source, ids_at, to):
        at = pl.multiple_of(ids[p, 0, ids_at] * FBW, FBW)
        message[p, :, to * FBW : (to + 1) * FBW] = source[:, pl.ds(at, FBW)]

    def item_blocks(p, carry):
        for k in range(kb):
            pick_one(p, item_table, first + k, k)
        return carry

    def user_blocks(p, carry):
        for k in range(nb * kb):
            pick_one(p, user_table, k, kb + k)
        pltpu.make_async_copy(message.at[p], out.at[p], sem).start()
        return carry

    lax.fori_loop(0, peers, item_blocks, 0)
    fetch_users.wait()
    lax.fori_loop(0, peers, user_blocks, 0)
    pltpu.make_async_copy(message, out, sem).wait()


def pick(ids, item_table, user_weights, first, nb, kb):
    shape = (ids.shape[0], item_table.shape[0], (1 + nb) * kb * FBW)
    return pl.pallas_call(
        functools.partial(pick_kernel, first, nb),
        out_shape=pltpu.HBM(shape, BF16),
        in_specs=[SMEM, VMEM, HBM],
        out_specs=HBM,
        scratch_shapes=[
            pltpu.VMEM(user_weights.shape, BF16),
            pltpu.VMEM(shape, BF16),
            pltpu.SemaphoreType.DMA,
            pltpu.SemaphoreType.DMA,
        ],
        compiler_params=params(10),
        name="pick",
    )(ids, item_table, in_hbm(user_weights))


def joined(vals):
    return jnp.concatenate([vals[k] for k in range(vals.shape[0])], axis=1)


def block_spec(vals, b):
    return pl.BlockSpec((1,) + vals.shape[1:], lambda i: (b, 0, 0, 0))


def part_spec(vals, cols, part):
    width = vals.shape[1] * FBW
    return pl.BlockSpec((cols.shape[0], cols.shape[1], width), lambda i: (0, 0, part))


def projected(vals, cols):
    peers, rp, width = cols.shape
    return lax.dot_general(
        joined(vals[0]),
        cols[...].reshape(peers * rp, width),
        (((1,), (1,)), ((), ())),
        preferred_element_type=F32,
    )


def project_kernel(vals, cols, *refs):
    own, send = refs[-2:]
    part = projected(vals, cols)
    own[...] = part
    send[...] = part.astype(BF16)


def project(vals, b, cols, part, follows=()):
    shape = (vals.shape[2], cols.shape[0] * cols.shape[1])
    return pl.pallas_call(
        project_kernel,
        out_shape=(jax.ShapeDtypeStruct(shape, F32), jax.ShapeDtypeStruct(shape, BF16)),
        grid=(1,),
        in_specs=[block_spec(vals, b), part_spec(vals, cols, part)]
        + [ANY] * len(follows),
        out_specs=(VMEM, VMEM),
        compiler_params=params(12),
        name="project",
    )(vals, cols, *follows)


def halves_kernel(feat, vals, cols, own, send):
    share = own.shape[0]
    part = projected(vals, cols)
    low, high = part[:share], part[share:]
    first = feat[0] == 0
    own[...] = jnp.where(first, low, high)
    send[...] = jnp.where(first, high, low).astype(BF16)


def project_halves(feat, vals, cols, part):
    share, rank = vals.shape[2] // 2, cols.shape[0] * cols.shape[1]
    return pl.pallas_call(
        halves_kernel,
        out_shape=(
            jax.ShapeDtypeStruct((share, rank), F32),
            jax.ShapeDtypeStruct((share, rank), BF16),
        ),
        grid=(1,),
        in_specs=[SMEM, block_spec(vals, 0), part_spec(vals, cols, part)],
        out_specs=(VMEM, VMEM),
        compiler_params=params(12),
        name="project_halves",
    )(feat, vals, cols)


def user_grad_kernel(vals, *refs):
    grads, out = refs[: 2 * vals.shape[0]], refs[-1]
    peers, rp, _ = out.shape
    kb = vals.shape[1]
    for b in range(vals.shape[0]):
        own, other = grads[2 * b], grads[2 * b + 1]
        grad = (own[...] + other[...].astype(F32)).astype(BF16)
        blocks = lax.dot_general(
            grad, joined(vals[b]), (((0,), (0,)), ((), ())), preferred_element_type=F32
        )
        out[:, :, b * kb * FBW : (b + 1) * kb * FBW] = blocks.astype(out.dtype).reshape(
            peers, rp, kb * FBW
        )


def user_grad_blocks(grads, vals, peers, follows):
    nb, kb, _, _ = vals.shape
    rank = grads[0].shape[1]
    shape = (peers, rank // peers, nb * kb * FBW)
    return pl.pallas_call(
        user_grad_kernel,
        out_shape=pltpu.HBM(shape, BF16),
        grid=(1,),
        in_specs=[VMEM] * (1 + len(grads)) + [ANY] * len(follows),
        out_specs=pl.BlockSpec(shape, lambda i: (0, 0, 0)),
        compiler_params=params(16),
        name="user_grad_blocks",
    )(vals, *grads, *follows)


def item_grad_kernel(grads, vals, out):
    peers, rp, width = out.shape
    blocks = jnp.dot(grads[...], joined(vals[0]), preferred_element_type=F32)
    out[...] = blocks.astype(out.dtype).reshape(peers, rp, width)


def item_grad_blocks(grads, vals, b, peers):
    _, kb, _, _ = vals.shape
    shape = (peers, grads.shape[0] // peers, kb * FBW)
    return pl.pallas_call(
        item_grad_kernel,
        out_shape=pltpu.HBM(shape, BF16),
        in_specs=[VMEM, block_spec(vals, b)],
        out_specs=pl.BlockSpec(shape, lambda i: (0, 0, 0)),
        grid=(1,),
        compiler_params=params(12),
        name="item_grad_blocks",
    )(grads, vals)


def collect_kernel(first, ids, back, out):
    peers, _, width = back.shape
    out[...] = jnp.zeros_like(out)

    def one(p, carry):
        for k in range(width // FBW):
            at = pl.multiple_of(ids[p, 0, first + k] * FBW, FBW)
            out[:, pl.ds(at, FBW)] += back[p, :, k * FBW : (k + 1) * FBW].astype(F32)
        return carry

    lax.fori_loop(0, peers, one, 0)


def collect(ids, back, first, columns):
    return pl.pallas_call(
        functools.partial(collect_kernel, first),
        out_shape=jax.ShapeDtypeStruct((back.shape[1], columns), F32),
        grid=(1,),
        in_specs=[SMEM, pl.BlockSpec(back.shape, lambda i: (0, 0, 0))],
        out_specs=VMEM,
        compiler_params=params(16),
        name="collect",
    )(ids, back)


def rating_columns(rated, g, share):
    if share % FBW == 0:
        return rated
    parts = FBW // share
    picked = rated[:, :share]
    for part in range(1, parts):
        picked = jnp.where(g % parts == part, rated[:, part * share : (part + 1) * share], picked)
    return picked


def place(k, bits):
    index = 0
    for bit in bits:
        index = 2 * index + (k & bit != 0)
    return k & 1, index


def rating_kernel(orders, rank_scale, grad_scale, me, observed, *refs):
    peers = 2 << len(orders[0])
    nb = observed.shape[0]
    parts, refs = refs[: 2 * nb], refs[2 * nb :]
    items, ratings, refs = refs[:peers], refs[peers], refs[peers + 1 :]
    grads, totals, refs = refs[: 2 * nb], refs[2 * nb : 2 * nb + 4], refs[2 * nb + 4 :]
    rated, table, sems, users, users_t, residuals = refs
    share = items[0].shape[0]
    tile, rank = parts[0].shape
    wide = rated.shape[2]
    width = 8

    def fetch(k):
        g = lax.bitwise_xor(me[0], k)
        at = pl.multiple_of(g * share // wide * wide, wide)
        return (
            pltpu.make_async_copy(ratings.at[:, pl.ds(at, wide)], rated.at[k], sems.at[0, k]),
            pltpu.make_async_copy(items[k], table.at[pl.ds(k * share, share), :], sems.at[1, k]),
        )

    for k in range(peers):
        for copy in fetch(k):
            copy.start()
    for b in range(nb):
        own, other = parts[2 * b], parts[2 * b + 1]
        rows = (own[...] + other[...].astype(F32)).astype(BF16)
        users[b * tile : (b + 1) * tile, :] = rows
        users_t[:, b * tile : (b + 1) * tile] = rows.T
    residuals[...] = jnp.zeros_like(residuals)
    for k in range(peers):
        g = lax.bitwise_xor(me[0], k)
        columns = pl.ds(k * share, share)
        for copy in fetch(k):
            copy.wait()
        def tiles(rows):
            predicted = lax.dot_general(
                users[rows, :], table[columns, :], (((1,), (1,)), ((), ())), preferred_element_type=F32
            )
            rating = rating_columns(rated[k, rows, :], g, share).astype(F32)
            residuals[rows, columns] = (predicted * rank_scale - rating).astype(BF16)

        seen = [observed[b, g] != 0 for b in range(nb)]
        all_seen = functools.reduce(jnp.logical_and, seen)
        pl.when(all_seen)(functools.partial(tiles, slice(0, nb * tile)))
        for b in range(nb):
            alone = jnp.logical_and(seen[b], jnp.logical_not(all_seen))
            pl.when(alone)(functools.partial(tiles, slice(b * tile, (b + 1) * tile)))

        if k % width == width - 1:
            start = k - width + 1
            terms = jnp.dot(
                users_t[...],
                residuals[:, pl.ds(start * share, width * share)],
                preferred_element_type=F32,
            )
            for j in range(width):
                term = terms[:, j * share : (j + 1) * share] * grad_scale
                for h, order in enumerate(orders):
                    group, index = place(start + j, order)
                    part = term[h * rank // 2 : (h + 1) * rank // 2]
                    totals[2 * h + group][index] = part.astype(BF16)
    step = tile // 4
    for b in range(nb):
        grad, grad_send = grads[2 * b], grads[2 * b + 1]
        for r in range(0, tile, step):
            part = jnp.dot(
                residuals[b * tile + r : b * tile + r + step, :],
                table[...],
                preferred_element_type=F32,
            )
            part = part * grad_scale
            grad[r : r + step, :] = part
            grad_send[r : r + step, :] = part.astype(BF16)


def in_hbm(array):
    return pltpu.with_memory_space_constraint(array, pltpu.HBM)


def rate(orders, me, observed, parts, items, ratings, rank_scale, grad_scale):
    peers = len(items)
    share, rank = items[0].shape
    nb = observed.shape[0]
    tile = parts[0].shape[0]
    quarter = jax.ShapeDtypeStruct((peers // 2, rank // 2, share), BF16)
    outs = [jax.ShapeDtypeStruct((tile, rank), F32), jax.ShapeDtypeStruct((tile, rank), BF16)]
    outs = outs * nb + [quarter] * 4
    return pl.pallas_call(
        functools.partial(rating_kernel, orders, rank_scale, grad_scale),
        out_shape=outs,
        in_specs=[SMEM, SMEM] + [VMEM] * (2 * nb) + [ANY] * peers + [HBM],
        out_specs=[VMEM] * len(outs),
        scratch_shapes=[
            pltpu.VMEM((peers, nb * tile, max(share, FBW)), BF16),
            pltpu.VMEM((peers * share, rank), BF16),
            pltpu.SemaphoreType.DMA((2, peers)),
            pltpu.VMEM((nb * tile, rank), BF16),
            pltpu.VMEM((rank, nb * tile), BF16),
            pltpu.VMEM((nb * tile, peers * share), BF16),
        ],
        compiler_params=params(36),
        name="rate",
    )(me, observed, *parts, *items, in_hbm(ratings))


def after_kernel(*refs):
    pass


def after(arrays, follows):
    n = len(arrays)
    return pl.pallas_call(
        after_kernel,
        out_shape=[pltpu.HBM(array.shape, array.dtype) for array in arrays],
        in_specs=[HBM] * n + [ANY] * len(follows),
        out_specs=[HBM] * n,
        input_output_aliases={i: i for i in range(n)},
        name="after",
    )(*map(in_hbm, arrays), *follows)


def across(n, bit):
    return [(i, i ^ bit) for i in range(n)]


def on_device(n_feat, n_rows, x_vals, x_blocks, y_vals, y_blocks, user_weights, item_weights, observed, ratings):
    x_vals, y_vals = x_vals[:, 0], y_vals[:, 0]
    nb, kbu, tile, _ = x_vals.shape
    ni, kbi, _, _ = y_vals.shape
    rank = user_weights.shape[0] * n_rows
    rank_scale = 1.0 / math.sqrt(rank)
    grad_scale = 1.0 / (tile * math.sqrt(rank))
    share = ni * tile // n_feat
    feat_id = lax.axis_index("feat")
    row_id = lax.axis_index("rows")

    def swap(array):
        return lax.ppermute(array, "feat", across(2, 1))

    def every(array):
        return lax.all_to_all(array, "rows", split_axis=0, concat_axis=0, tiled=True)

    def feat_sum(own, send):
        if n_feat == 2:
            return own, swap(send)
        return lax.psum(own, "feat"), jnp.zeros_like(send)

    ids = every(ask(x_blocks, y_blocks, n_rows))
    (item_table,) = preload(item_weights)
    cols = every(pick(ids, item_table, user_weights, nb * kbu, nb, kbu))
    if n_feat == 2:
        feat = feat_id.reshape(1).astype(jnp.int32)
        own, send = project_halves(feat, y_vals, cols, 0)
        item_share = (own + swap(send).astype(F32)).astype(BF16)
    else:
        own, send = project(y_vals, 0, cols, 0)
        item_share = lax.psum_scatter(own, "feat", scatter_dimension=0, tiled=True).astype(BF16)
    parts = []
    for b in range(nb):
        parts.extend(feat_sum(*project(x_vals, b, cols, 1 + b, (send,))))

    items = {0: item_share}
    bit = n_rows // 2
    while bit:
        for k in list(items):
            items[k + bit] = lax.ppermute(items[k], "rows", across(n_rows, bit))
        bit //= 2
    items = [items[k] for k in range(n_rows)]

    me = row_id.reshape(1).astype(jnp.int32)
    bits = [1 << i for i in range(1, n_rows.bit_length() - 1)]
    orders = [bits, bits[1:2] + bits[:1] + bits[2:]]
    *grads, first, first_give, second, second_give = rate(
        orders, me, observed, parts, items, ratings[:, 0], rank_scale, grad_scale
    )
    grads = [part for b in range(nb) for part in feat_sum(*grads[2 * b : 2 * b + 2])]

    def plus(a, b):
        return (a.astype(F32) + b.astype(F32)).astype(BF16)

    def give(array, bit):
        return lax.ppermute(array, "rows", across(n_rows, bit))

    sums = [plus(first, give(first_give, 1)), plus(second, give(second_give, 1))]
    for step in range(len(bits)):
        for h, order in enumerate(orders):
            half = sums[h].shape[0] // 2
            sums[h] = plus(sums[h][:half], give(sums[h][half:], order[step]))
        if step == len(bits) - 2:
            user_ask = user_grad_blocks(grads, x_vals, n_rows, sums)
    item_grad = jnp.concatenate([part[0] for part in sums])
    user_back = in_hbm(every(*after([user_ask], sums)))
    if n_feat == 2:
        other = swap(item_grad)
        first = feat_id == 0
        item_grad = jnp.concatenate(
            [jnp.where(first, item_grad, other), jnp.where(first, other, item_grad)], axis=1
        )
    else:
        item_grad = lax.all_gather(item_grad, "feat", axis=1, tiled=True)
    item_back = every(*after([item_grad_blocks(item_grad, y_vals, 0, n_rows)], [user_back]))

    return (
        collect(ids, user_back, 0, user_weights.shape[1]),
        collect(ids, item_back, nb * kbu, item_weights.shape[1]),
    )


def solution(mesh):
    return jax.shard_map(
        functools.partial(on_device, mesh.shape["feat"], mesh.shape["rows"]),
        mesh=mesh,
        in_specs=(
            P("rows", "feat", None, None, None),
            P("rows", "feat", None),
            P("rows", "feat", None, None, None),
            P("rows", "feat", None),
            P("rows", "feat"),
            P("rows", "feat"),
            P("rows", None),
            P("rows", "feat", None),
        ),
        out_specs=(P("rows", "feat"), P("rows", "feat")),
        check_vma=False,
    )
```

```python
import functools
import math

import jax
import jax.numpy as jnp
from jax import lax
from jax.experimental import pallas as pl
from jax.experimental.pallas import tpu as pltpu
from jax.sharding import PartitionSpec as P

FBW = 128
F32 = jnp.float32
BF16 = jnp.bfloat16
VMEM = pl.BlockSpec(memory_space=pltpu.VMEM)
SMEM = pl.BlockSpec(memory_space=pltpu.SMEM)
HBM = pl.BlockSpec(memory_space=pltpu.HBM)
ANY = pl.BlockSpec(memory_space=pl.ANY)


def params(mib):
    return pltpu.CompilerParams(vmem_limit_bytes=mib * 1024 * 1024)


def ask_kernel(x_blocks, y_blocks, out):
    rows = [x_blocks[b] for b in range(x_blocks.shape[0])]
    rows += [y_blocks[b] for b in range(y_blocks.shape[0])]
    used = sum(row.shape[1] for row in rows)
    rows.append(jnp.zeros((1, out.shape[2] - used), jnp.int32))
    out[...] = jnp.broadcast_to(jnp.concatenate(rows, axis=1)[None], out.shape)


def ask(x_blocks, y_blocks, peers):
    return pl.pallas_call(
        ask_kernel,
        out_shape=jax.ShapeDtypeStruct((peers, 1, FBW), jnp.int32),
        in_specs=[VMEM, VMEM],
        out_specs=VMEM,
        name="ask",
    )(x_blocks, y_blocks)


def preload_kernel(*refs):
    n = len(refs) // 2
    sems = refs[-1]
    copies = [
        pltpu.make_async_copy(refs[i], refs[n + i], sems.at[i]) for i in range(n)
    ]
    for copy in copies:
        copy.start()
    for copy in copies:
        copy.wait()


def preload(*arrays):
    return pl.pallas_call(
        preload_kernel,
        out_shape=[pltpu.VMEM(array.shape, array.dtype) for array in arrays],
        in_specs=[HBM] * len(arrays),
        out_specs=[VMEM] * len(arrays),
        scratch_shapes=[pltpu.SemaphoreType.DMA((len(arrays),))],
        compiler_params=params(12),
        name="preload",
    )(*[in_hbm(array) for array in arrays])


def pick_kernel(first, nb, ids, item_table, user_weights, out, user_table, message, sem, table_sem):
    peers, _, width = out.shape
    kb = width // FBW // (1 + nb)
    fetch_users = pltpu.make_async_copy(user_weights, user_table, table_sem)
    fetch_users.start()

    def pick_one(p, source, ids_at, to):
        at = pl.multiple_of(ids[p, 0, ids_at] * FBW, FBW)
        message[p, :, to * FBW : (to + 1) * FBW] = source[:, pl.ds(at, FBW)]

    def item_blocks(p, carry):
        for k in range(kb):
            pick_one(p, item_table, first + k, k)
        return carry

    def user_blocks(p, carry):
        for k in range(nb * kb):
            pick_one(p, user_table, k, kb + k)
        pltpu.make_async_copy(message.at[p], out.at[p], sem).start()
        return carry

    lax.fori_loop(0, peers, item_blocks, 0)
    fetch_users.wait()
    lax.fori_loop(0, peers, user_blocks, 0)
    pltpu.make_async_copy(message, out, sem).wait()


def pick(ids, item_table, user_weights, first, nb, kb):
    shape = (ids.shape[0], item_table.shape[0], (1 + nb) * kb * FBW)
    return pl.pallas_call(
        functools.partial(pick_kernel, first, nb),
        out_shape=pltpu.HBM(shape, BF16),
        in_specs=[SMEM, VMEM, HBM],
        out_specs=HBM,
        scratch_shapes=[
            pltpu.VMEM(user_weights.shape, BF16),
            pltpu.VMEM(shape, BF16),
            pltpu.SemaphoreType.DMA,
            pltpu.SemaphoreType.DMA,
        ],
        compiler_params=params(10),
        name="pick",
    )(ids, item_table, in_hbm(user_weights))


def joined(vals):
    return jnp.concatenate([vals[k] for k in range(vals.shape[0])], axis=1)


def block_spec(vals, b):
    return pl.BlockSpec((1,) + vals.shape[1:], lambda i: (b, 0, 0, 0))


def part_spec(vals, cols, part):
    width = vals.shape[1] * FBW
    return pl.BlockSpec((cols.shape[0], cols.shape[1], width), lambda i: (0, 0, part))


def projected(vals, cols):
    peers, rp, width = cols.shape
    return lax.dot_general(
        joined(vals[0]),
        cols[...].reshape(peers * rp, width),
        (((1,), (1,)), ((), ())),
        preferred_element_type=F32,
    )


def project_kernel(vals, cols, *refs):
    own, send = refs[-2:]
    part = projected(vals, cols)
    own[...] = part
    send[...] = part.astype(BF16)


def project(vals, b, cols, part, follows=()):
    shape = (vals.shape[2], cols.shape[0] * cols.shape[1])
    return pl.pallas_call(
        project_kernel,
        out_shape=(jax.ShapeDtypeStruct(shape, F32), jax.ShapeDtypeStruct(shape, BF16)),
        grid=(1,),
        in_specs=[block_spec(vals, b), part_spec(vals, cols, part)]
        + [ANY] * len(follows),
        out_specs=(VMEM, VMEM),
        compiler_params=params(12),
        name="project",
    )(vals, cols, *follows)


def halves_kernel(feat, vals, cols, own, send):
    share = own.shape[0]
    part = projected(vals, cols)
    low, high = part[:share], part[share:]
    first = feat[0] == 0
    own[...] = jnp.where(first, low, high)
    send[...] = jnp.where(first, high, low).astype(BF16)


def project_halves(feat, vals, cols, part):
    share, rank = vals.shape[2] // 2, cols.shape[0] * cols.shape[1]
    return pl.pallas_call(
        halves_kernel,
        out_shape=(
            jax.ShapeDtypeStruct((share, rank), F32),
            jax.ShapeDtypeStruct((share, rank), BF16),
        ),
        grid=(1,),
        in_specs=[SMEM, block_spec(vals, 0), part_spec(vals, cols, part)],
        out_specs=(VMEM, VMEM),
        compiler_params=params(12),
        name="project_halves",
    )(feat, vals, cols)


def user_grad_kernel(vals, *refs):
    grads, out = refs[: 2 * vals.shape[0]], refs[-1]
    peers, rp, _ = out.shape
    kb = vals.shape[1]
    for b in range(vals.shape[0]):
        own, other = grads[2 * b], grads[2 * b + 1]
        grad = (own[...] + other[...].astype(F32)).astype(BF16)
        blocks = lax.dot_general(
            grad, joined(vals[b]), (((0,), (0,)), ((), ())), preferred_element_type=F32
        )
        out[:, :, b * kb * FBW : (b + 1) * kb * FBW] = blocks.astype(out.dtype).reshape(
            peers, rp, kb * FBW
        )


def user_grad_blocks(grads, vals, peers, follows):
    nb, kb, _, _ = vals.shape
    rank = grads[0].shape[1]
    shape = (peers, rank // peers, nb * kb * FBW)
    return pl.pallas_call(
        user_grad_kernel,
        out_shape=pltpu.HBM(shape, BF16),
        grid=(1,),
        in_specs=[VMEM] * (1 + len(grads)) + [ANY] * len(follows),
        out_specs=pl.BlockSpec(shape, lambda i: (0, 0, 0)),
        compiler_params=params(16),
        name="user_grad_blocks",
    )(vals, *grads, *follows)


def item_grad_kernel(grads, vals, out):
    peers, rp, width = out.shape
    blocks = jnp.dot(grads[...], joined(vals[0]), preferred_element_type=F32)
    out[...] = blocks.astype(out.dtype).reshape(peers, rp, width)


def item_grad_blocks(grads, vals, b, peers):
    _, kb, _, _ = vals.shape
    shape = (peers, grads.shape[0] // peers, kb * FBW)
    return pl.pallas_call(
        item_grad_kernel,
        out_shape=pltpu.HBM(shape, BF16),
        in_specs=[VMEM, block_spec(vals, b)],
        out_specs=pl.BlockSpec(shape, lambda i: (0, 0, 0)),
        grid=(1,),
        compiler_params=params(12),
        name="item_grad_blocks",
    )(grads, vals)


def collect_kernel(first, ids, back, out):
    peers, _, width = back.shape
    out[...] = jnp.zeros_like(out)

    def one(p, carry):
        for k in range(width // FBW):
            at = pl.multiple_of(ids[p, 0, first + k] * FBW, FBW)
            out[:, pl.ds(at, FBW)] += back[p, :, k * FBW : (k + 1) * FBW].astype(F32)
        return carry

    lax.fori_loop(0, peers, one, 0)


def collect(ids, back, first, columns):
    return pl.pallas_call(
        functools.partial(collect_kernel, first),
        out_shape=jax.ShapeDtypeStruct((back.shape[1], columns), F32),
        grid=(1,),
        in_specs=[SMEM, pl.BlockSpec(back.shape, lambda i: (0, 0, 0))],
        out_specs=VMEM,
        compiler_params=params(16),
        name="collect",
    )(ids, back)


def rating_columns(rated, g, share):
    if share % FBW == 0:
        return rated
    parts = FBW // share
    picked = rated[:, :share]
    for part in range(1, parts):
        picked = jnp.where(g % parts == part, rated[:, part * share : (part + 1) * share], picked)
    return picked


def place(k, bits):
    index = 0
    for bit in bits:
        index = 2 * index + (k & bit != 0)
    return k & 1, index


def rating_kernel(orders, rank_scale, grad_scale, me, observed, *refs):
    peers = 2 << len(orders[0])
    nb = observed.shape[0]
    parts, refs = refs[: 2 * nb], refs[2 * nb :]
    items, ratings, refs = refs[:peers], refs[peers], refs[peers + 1 :]
    grads, totals, refs = refs[: 2 * nb], refs[2 * nb : 2 * nb + 4], refs[2 * nb + 4 :]
    rated, table, sems, users, users_t, residuals = refs
    share = items[0].shape[0]
    tile, rank = parts[0].shape
    wide = rated.shape[2]
    width = 8

    def fetch(k):
        g = lax.bitwise_xor(me[0], k)
        at = pl.multiple_of(g * share // wide * wide, wide)
        return (
            pltpu.make_async_copy(ratings.at[:, pl.ds(at, wide)], rated.at[k], sems.at[0, k]),
            pltpu.make_async_copy(items[k], table.at[pl.ds(k * share, share), :], sems.at[1, k]),
        )

    for k in range(peers):
        for copy in fetch(k):
            copy.start()
    for b in range(nb):
        own, other = parts[2 * b], parts[2 * b + 1]
        rows = (own[...] + other[...].astype(F32)).astype(BF16)
        users[b * tile : (b + 1) * tile, :] = rows
        users_t[:, b * tile : (b + 1) * tile] = rows.T
    residuals[...] = jnp.zeros_like(residuals)
    for k in range(peers):
        g = lax.bitwise_xor(me[0], k)
        columns = pl.ds(k * share, share)
        for copy in fetch(k):
            copy.wait()
        def tiles(rows):
            predicted = lax.dot_general(
                users[rows, :], table[columns, :], (((1,), (1,)), ((), ())), preferred_element_type=F32
            )
            rating = rating_columns(rated[k, rows, :], g, share).astype(F32)
            residuals[rows, columns] = (predicted * rank_scale - rating).astype(BF16)

        seen = [observed[b, g] != 0 for b in range(nb)]
        all_seen = functools.reduce(jnp.logical_and, seen)
        pl.when(all_seen)(functools.partial(tiles, slice(0, nb * tile)))
        for b in range(nb):
            alone = jnp.logical_and(seen[b], jnp.logical_not(all_seen))
            pl.when(alone)(functools.partial(tiles, slice(b * tile, (b + 1) * tile)))

        if k % width == width - 1:
            start = k - width + 1
            terms = jnp.dot(
                users_t[...],
                residuals[:, pl.ds(start * share, width * share)],
                preferred_element_type=F32,
            )
            for j in range(width):
                term = terms[:, j * share : (j + 1) * share] * grad_scale
                for h, order in enumerate(orders):
                    group, index = place(start + j, order)
                    part = term[h * rank // 2 : (h + 1) * rank // 2]
                    totals[2 * h + group][index] = part.astype(BF16)
    step = tile // 4
    for b in range(nb):
        grad, grad_send = grads[2 * b], grads[2 * b + 1]
        for r in range(0, tile, step):
            part = jnp.dot(
                residuals[b * tile + r : b * tile + r + step, :],
                table[...],
                preferred_element_type=F32,
            )
            part = part * grad_scale
            grad[r : r + step, :] = part
            grad_send[r : r + step, :] = part.astype(BF16)


def in_hbm(array):
    return pltpu.with_memory_space_constraint(array, pltpu.HBM)


def rate(orders, me, observed, parts, items, ratings, rank_scale, grad_scale):
    peers = len(items)
    share, rank = items[0].shape
    nb = observed.shape[0]
    tile = parts[0].shape[0]
    quarter = jax.ShapeDtypeStruct((peers // 2, rank // 2, share), BF16)
    outs = [jax.ShapeDtypeStruct((tile, rank), F32), jax.ShapeDtypeStruct((tile, rank), BF16)]
    outs = outs * nb + [quarter] * 4
    return pl.pallas_call(
        functools.partial(rating_kernel, orders, rank_scale, grad_scale),
        out_shape=outs,
        in_specs=[SMEM, SMEM] + [VMEM] * (2 * nb) + [ANY] * peers + [HBM],
        out_specs=[VMEM] * len(outs),
        scratch_shapes=[
            pltpu.VMEM((peers, nb * tile, max(share, FBW)), BF16),
            pltpu.VMEM((peers * share, rank), BF16),
            pltpu.SemaphoreType.DMA((2, peers)),
            pltpu.VMEM((nb * tile, rank), BF16),
            pltpu.VMEM((rank, nb * tile), BF16),
            pltpu.VMEM((nb * tile, peers * share), BF16),
        ],
        compiler_params=params(36),
        name="rate",
    )(me, observed, *parts, *items, in_hbm(ratings))


def after_kernel(*refs):
    pass


def after(arrays, follows):
    n = len(arrays)
    return pl.pallas_call(
        after_kernel,
        out_shape=[pltpu.HBM(array.shape, array.dtype) for array in arrays],
        in_specs=[HBM] * n + [ANY] * len(follows),
        out_specs=[HBM] * n,
        input_output_aliases={i: i for i in range(n)},
        name="after",
    )(*map(in_hbm, arrays), *follows)


def across(n, bit):
    return [(i, i ^ bit) for i in range(n)]


def on_device(n_feat, n_rows, x_vals, x_blocks, y_vals, y_blocks, user_weights, item_weights, observed, ratings):
    x_vals, y_vals = x_vals[:, 0], y_vals[:, 0]
    nb, kbu, tile, _ = x_vals.shape
    ni, kbi, _, _ = y_vals.shape
    rank = user_weights.shape[0] * n_rows
    rank_scale = 1.0 / math.sqrt(rank)
    grad_scale = 1.0 / (tile * math.sqrt(rank))
    share = ni * tile // n_feat
    feat_id = lax.axis_index("feat")
    row_id = lax.axis_index("rows")

    def swap(array):
        return lax.ppermute(array, "feat", across(2, 1))

    def every(array):
        return lax.all_to_all(array, "rows", split_axis=0, concat_axis=0, tiled=True)

    def feat_sum(own, send):
        if n_feat == 2:
            return own, swap(send)
        return lax.psum(own, "feat"), jnp.zeros_like(send)

    ids = every(ask(x_blocks, y_blocks, n_rows))
    (item_table,) = preload(item_weights)
    cols = every(pick(ids, item_table, user_weights, nb * kbu, nb, kbu))
    if n_feat == 2:
        feat = feat_id.reshape(1).astype(jnp.int32)
        own, send = project_halves(feat, y_vals, cols, 0)
        item_share = (own + swap(send).astype(F32)).astype(BF16)
    else:
        own, send = project(y_vals, 0, cols, 0)
        item_share = lax.psum_scatter(own, "feat", scatter_dimension=0, tiled=True).astype(BF16)
    parts = []
    for b in range(nb):
        parts.extend(feat_sum(*project(x_vals, b, cols, 1 + b, (send,))))

    items = {0: item_share}
    bit = n_rows // 2
    while bit:
        for k in list(items):
            items[k + bit] = lax.ppermute(items[k], "rows", across(n_rows, bit))
        bit //= 2
    items = [items[k] for k in range(n_rows)]

    me = row_id.reshape(1).astype(jnp.int32)
    bits = [1 << i for i in range(1, n_rows.bit_length() - 1)]
    orders = [bits, bits[1:2] + bits[:1] + bits[2:]]
    *grads, first, first_give, second, second_give = rate(
        orders, me, observed, parts, items, ratings[:, 0], rank_scale, grad_scale
    )
    grads = [part for b in range(nb) for part in feat_sum(*grads[2 * b : 2 * b + 2])]

    def plus(a, b):
        return (a.astype(F32) + b.astype(F32)).astype(BF16)

    def give(array, bit):
        return lax.ppermute(array, "rows", across(n_rows, bit))

    sums = [plus(first, give(first_give, 1)), plus(second, give(second_give, 1))]
    sent = [None] * len(orders)
    for step in range(len(bits)):
        for h, order in enumerate(orders):
            half = sums[h].shape[0] // 2
            sent[h] = give(sums[h][half:], order[step])
            sums[h] = plus(sums[h][:half], sent[h])
        if step == len(bits) - 2:
            user_ask = user_grad_blocks(grads, x_vals, n_rows, sums)
    item_grad = jnp.concatenate([part[0] for part in sums])
    user_back = in_hbm(every(*after([user_ask], sent)))
    if n_feat == 2:
        other = swap(item_grad)
        first = feat_id == 0
        item_grad = jnp.concatenate(
            [jnp.where(first, item_grad, other), jnp.where(first, other, item_grad)], axis=1
        )
    else:
        item_grad = lax.all_gather(item_grad, "feat", axis=1, tiled=True)
    item_back = every(*after([item_grad_blocks(item_grad, y_vals, 0, n_rows)], [user_back]))

    return (
        collect(ids, user_back, 0, user_weights.shape[1]),
        collect(ids, item_back, nb * kbu, item_weights.shape[1]),
    )


def solution(mesh):
    return jax.shard_map(
        functools.partial(on_device, mesh.shape["feat"], mesh.shape["rows"]),
        mesh=mesh,
        in_specs=(
            P("rows", "feat", None, None, None),
            P("rows", "feat", None),
            P("rows", "feat", None, None, None),
            P("rows", "feat", None),
            P("rows", "feat"),
            P("rows", "feat"),
            P("rows", None),
            P("rows", "feat", None),
        ),
        out_specs=(P("rows", "feat"), P("rows", "feat")),
        check_vma=False,
    )
```
